128 devices in a mesh: seq: 32 (over z, y_hi, x), chan: 4 (over y_lo, core).
Axes of the slice: x: 4, y: 4 (y_hi: 2, y_lo: 2; y = y_hi * 2 + y_lo), z: 4, core: 2. Of those that a mesh axis runs over, the one named last changes fastest.
Arguments:
- tokens: bfloat16 [131072, 4096], P('seq', 'chan'), may hold values from -170 to 170
- norm_gain: bfloat16 [4096], P('chan'), may hold values from 0.099609375 to 1.8984375
- first_factor: bfloat16 [512, 512], replicated, may hold values from -0.25 to 0.25
- twiddle_in: bfloat16 [256, 512], P('seq'), may hold values from -4 to 4
- second_factor: bfloat16 [256, 256], replicated, may hold values from -0.375 to 0.375
- kernel_gate: bfloat16 [256, 512, 4096], P(None, 'seq', 'chan'), may hold values from -4 to 4
- second_inverse: bfloat16 [256, 256], replicated, may hold values from -0.375 to 0.375
- twiddle_out: bfloat16 [256, 512], P(None, 'seq'), may hold values from -4 to 4
- first_inverse: bfloat16 [512, 512], replicated, may hold values from -0.25 to 0.25
Outputs:
- mixed: bfloat16 [131072, 4096], P('seq', 'chan')
The draws below stay inside these ranges and needn't reach their ends.
All inputs are finite; a program needn't handle non-finite values.
Results may differ from the reference program's by a relative error of at most 0.007.
Values may be sent and summed in bfloat16 or wider, within the bound.
No kernel may reach another device: no remote copies, remote signals or barrier semaphores. Data moves between devices by JAX's collectives and lax.ppermute only.
A program may use at most 192 MiB of HBM per device.

```python
import jax
import jax.numpy as jnp
from jax import lax

D = 4096
P_SIZE = 256
Q = 512


def draw_tokens(key, part):
    key = jax.random.fold_in(key, 11)
    keys = jax.random.split(key, 2)
    column = jnp.arange(D, dtype=jnp.float32) / D
    spread = jnp.power(10.0, 0.8 * column + 0.2 * jax.random.uniform(keys[1], (D,), jnp.float32))
    values = jnp.clip(jax.random.normal(keys[0], (P_SIZE * Q, D), jnp.float32), -4.0, 4.0) * spread
    return values.astype(jnp.bfloat16)


def block_levels(key, extent, shards, low, high):
    def one(dim, shards_of):
        draws = jax.random.uniform(jax.random.fold_in(jax.random.fold_in(key, 6), dim), (shards_of,), jnp.float32, low / len(shards), high / len(shards))
        return jnp.repeat(jnp.exp(draws), extent[dim] // shards_of).reshape((-1,) + (1,) * (len(extent) - dim - 1))

    loudness = one(*shards[0])
    for cut in shards[1:]:
        loudness = loudness * one(*cut)
    return loudness


def noise(stream_key, shape, scale, most, shards=(), kind=jnp.bfloat16):
    values = jax.random.normal(stream_key, shape, jnp.float32) * scale
    if len(shards) > 0:
        values = block_levels(stream_key, shape, shards, -0.22, 0.18) * values
    return jnp.clip(values, min=-most, max=most).astype(kind)


def setup_inputs(seed: int = 0) -> dict:
    streams_of = jax.random.split(jax.random.key(seed), 10)
    tokens = draw_tokens(jax.random.fold_in(streams_of[9], 71), 0)
    norm_gain = jnp.clip(1.0 + 0.18 * jax.random.normal(streams_of[1], (D,), jnp.float32), 0.099609375, 1.8984375).astype(jnp.bfloat16)
    first_factor = noise(streams_of[2], (Q, Q), Q ** -0.5, 0.25)
    twiddle_in = noise(streams_of[3], (P_SIZE, Q), 1.0, 4.0, ((0, 32),))
    second_factor = noise(streams_of[4], (P_SIZE, P_SIZE), P_SIZE ** -0.5, 0.375)
    kernel_gate = noise(streams_of[5], (P_SIZE, Q, D), 1.0, 4.0, ((1, 32), (2, 4)))
    second_inverse = noise(streams_of[6], (P_SIZE, P_SIZE), P_SIZE ** -0.5, 0.375)
    twiddle_out = noise(streams_of[7], (P_SIZE, Q), 1.0, 4.0, ((1, 32),))
    first_inverse = noise(streams_of[8], (Q, Q), Q ** -0.5, 0.25)
    return {"tokens": tokens, "norm_gain": norm_gain, "first_factor": first_factor, "twiddle_in": twiddle_in, "second_factor": second_factor, "kernel_gate": kernel_gate, "second_inverse": second_inverse, "twiddle_out": twiddle_out, "first_inverse": first_inverse}


def monarch_block(values, inverse_rms, gain, gate_block, first_factor, twiddle_in, second_factor, second_inverse, twiddle_out, first_inverse):
    normed = (values.astype(jnp.float32) * inverse_rms[:, :, None] * gain.astype(jnp.float32)).astype(jnp.bfloat16)
    first = jnp.einsum('kq,pqc->pkc', first_factor.astype(jnp.float32), normed.astype(jnp.float32))
    first = (first * twiddle_in.astype(jnp.float32)[:, :, None]).astype(jnp.bfloat16)
    gated = jnp.einsum('mp,pkc->mkc', second_factor.astype(jnp.float32), first.astype(jnp.float32))
    gated = (gated * gate_block.astype(jnp.float32)).astype(jnp.bfloat16)
    back = jnp.einsum('nm,mkc->nkc', second_inverse.astype(jnp.float32), gated.astype(jnp.float32))
    back = (back * twiddle_out.astype(jnp.float32)[:, :, None]).astype(jnp.bfloat16)
    result = jnp.einsum('qk,nkc->nqc', first_inverse.astype(jnp.float32), back.astype(jnp.float32))
    return result.astype(jnp.bfloat16)

def reference(tokens, norm_gain, first_factor, twiddle_in, second_factor, kernel_gate, second_inverse, twiddle_out, first_inverse):
    widened = tokens.astype(jnp.float32)
    square = lax.optimization_barrier(jnp.sum(widened * widened, axis=1))
    inverse_rms = lax.rsqrt(square / D + 1e-05).reshape(P_SIZE, Q)
    channel_width = min(D, 256)
    count_blocks = D // channel_width
    stacked = tokens.reshape(P_SIZE, Q, count_blocks, channel_width).transpose(2, 0, 1, 3)
    gate_stack = kernel_gate.reshape(P_SIZE, Q, count_blocks, channel_width).transpose(2, 0, 1, 3)
    gain_stack = norm_gain.reshape(count_blocks, channel_width)

    def process(pieces):
        return monarch_block(pieces[0], inverse_rms, pieces[1], pieces[2], first_factor, twiddle_in, second_factor, second_inverse, twiddle_out, first_inverse)
    result = lax.map(process, (stacked, gain_stack, gate_stack))
    return result.transpose(1, 2, 0, 3).reshape(P_SIZE * Q, D)
```

```python
import functools

import jax
import jax.numpy as jnp
from jax import lax
from jax.experimental import pallas as pl
from jax.experimental.pallas import tpu as pltpu
from jax.sharding import PartitionSpec as P

CHUNKS = 2
VMEM_LIMIT = 56 * 1024 * 1024


def params():
    return pltpu.CompilerParams(
        dimension_semantics=("arbitrary",), vmem_limit_bytes=VMEM_LIMIT
    )


def first_kernel(p_block, x_ref, inv_ref, gain_ref, factor_ref, tw_ref, out_ref, held):
    step = pl.program_id(0)
    order = factor_ref.shape[0]

    @pl.when(step < p_block)
    def _():
        scaled = (factor_ref[...] * inv_ref[0]).astype(jnp.bfloat16)
        result = jnp.dot(scaled, x_ref[...], preferred_element_type=jnp.float32)
        result = result * tw_ref[0] * gain_ref[...]
        for part in range(held.shape[0]):
            held[part, pl.ds(step, order, stride=p_block), :] = result[
                :, part * 128 : (part + 1) * 128
            ]

    @pl.when(step >= p_block)
    def _():
        rows = out_ref.shape[0]
        base = pl.multiple_of((step - p_block) * rows, rows)
        for part in range(held.shape[0]):
            out_ref[:, part * 128 : (part + 1) * 128] = held[
                part, pl.ds(base, rows), :
            ].astype(jnp.bfloat16)


def first_call(tokens, inv, gain, factor, tw, chunk, width):
    rows, _ = tokens.shape
    p_block, _, order = inv.shape
    parts = 8
    out_rows = rows // parts
    return pl.pallas_call(
        functools.partial(first_kernel, p_block),
        grid=(p_block + parts,),
        in_specs=[
            pl.BlockSpec((order, width), lambda i: (jnp.minimum(i, p_block - 1), chunk)),
            pl.BlockSpec((1, 1, order), lambda i: (jnp.minimum(i, p_block - 1), 0, 0)),
            pl.BlockSpec((1, width), lambda i: (0, chunk)),
            pl.BlockSpec((order, order), lambda i: (0, 0)),
            pl.BlockSpec((1, order, 1), lambda i: (jnp.minimum(i, p_block - 1), 0, 0)),
        ],
        out_specs=pl.BlockSpec((out_rows, width), lambda i: (jnp.maximum(i - p_block, 0), 0)),
        out_shape=jax.ShapeDtypeStruct((rows, width), jnp.bfloat16),
        scratch_shapes=[pltpu.VMEM((width // 128, rows, 128), jnp.float32)],
        compiler_params=params(),
        cost_estimate=pl.CostEstimate(
            flops=2 * rows * order * width, bytes_accessed=4 * rows * width, transcendentals=0
        ),
        name="first_section",
    )(tokens, inv, gain, factor, tw)


def middle_kernel(pairs, v_ref, pair_ref, gate_ref, inverse_ref, tw_ref, out_ref, held):
    step = pl.program_id(0)
    groups, _, width = v_ref.shape
    m_order = inverse_ref.shape[0]

    @pl.when(step < pairs)
    def _():
        values = v_ref[...].reshape(groups * 16, width)
        gated = jnp.dot(pair_ref[...], values, preferred_element_type=jnp.float32)
        for one in range(2):
            half = gated[one * m_order : (one + 1) * m_order]
            half = (half * gate_ref[one].astype(jnp.float32)).astype(jnp.bfloat16)
            back = jnp.dot(inverse_ref[...], half, preferred_element_type=jnp.float32)
            back = back * tw_ref[one]
            for part in range(held.shape[0]):
                held[part, pl.ds(2 * step + one, m_order, stride=2 * pairs), :] = back[
                    :, part * 128 : (part + 1) * 128
                ]

    @pl.when(step >= pairs)
    def _():
        rows = out_ref.shape[0]
        base = pl.multiple_of((step - pairs) * rows, rows)
        for part in range(held.shape[0]):
            out_ref[:, part * 128 : (part + 1) * 128] = held[
                part, pl.ds(base, rows), :
            ].astype(jnp.bfloat16)


def middle_call(values, pair, gate, inverse, tw, chunk):
    groups, depth, width = values.shape
    pairs = depth // 16
    m_order = inverse.shape[0]
    rows = groups * depth
    parts = 8
    last = pairs - 1
    return pl.pallas_call(
        functools.partial(middle_kernel, pairs),
        grid=(pairs + parts,),
        in_specs=[
            pl.BlockSpec((groups, 16, width), lambda i: (0, jnp.minimum(i, last), 0)),
            pl.BlockSpec((2 * m_order, 2 * m_order), lambda i: (0, 0)),
            pl.BlockSpec((2, m_order, width), lambda i: (jnp.minimum(i, last), 0, chunk)),
            pl.BlockSpec((m_order, m_order), lambda i: (0, 0)),
            pl.BlockSpec((2, m_order, 1), lambda i: (jnp.minimum(i, last), 0, 0)),
        ],
        out_specs=pl.BlockSpec((rows // parts, width), lambda i: (jnp.maximum(i - pairs, 0), 0)),
        out_shape=jax.ShapeDtypeStruct((rows, width), jnp.bfloat16),
        scratch_shapes=[pltpu.VMEM((width // 128, rows, 128), jnp.float32)],
        compiler_params=params(),
        cost_estimate=pl.CostEstimate(
            flops=6 * rows * m_order * width, bytes_accessed=6 * rows * width, transcendentals=0
        ),
        name="middle_section",
    )(values, pair, gate, inverse, tw)


def last_kernel(v_ref, factor_ref, *rest):
    out_ref = rest[-1]
    groups, depth, width = v_ref.shape
    values = v_ref[...].reshape(groups * depth, width)
    out_ref[...] = jnp.dot(factor_ref[...], values, preferred_element_type=jnp.float32).astype(
        jnp.bfloat16
    )


def last_call(values, factor, so_far, chunk, full_width):
    groups, depth, width = values.shape
    order = factor.shape[0]
    per = order // groups
    blocks = depth // per
    in_specs = [
        pl.BlockSpec((groups, per, width), lambda i: (0, i, 0)),
        pl.BlockSpec((order, order), lambda i: (0, 0)),
    ]
    operands = [values, factor]
    aliases = {}
    if so_far is not None:
        in_specs.append(pl.BlockSpec(memory_space=pl.ANY))
        operands.append(so_far)
        aliases = {2: 0}
    return pl.pallas_call(
        last_kernel,
        grid=(blocks,),
        in_specs=in_specs,
        out_specs=pl.BlockSpec((order, width), lambda i: (i, chunk)),
        out_shape=jax.ShapeDtypeStruct((blocks * order, full_width), jnp.bfloat16),
        input_output_aliases=aliases,
        compiler_params=params(),
        cost_estimate=pl.CostEstimate(
            flops=2 * blocks * order * order * width,
            bytes_accessed=4 * blocks * order * width,
            transcendentals=0,
        ),
        name="last_section",
    )(*operands)


def per_device(
    tokens,
    norm_gain,
    first_factor,
    twiddle_in,
    second_factor,
    kernel_gate,
    second_inverse,
    twiddle_out,
    first_inverse,
):
    f32 = jnp.float32
    seq_count = lax.axis_size("seq")
    rows_dev, width_dev = tokens.shape
    q_order = first_factor.shape[0]
    p_order = second_factor.shape[0]
    p_block = p_order // seq_count
    k_block = q_order // seq_count
    width = width_dev // CHUNKS

    widened = tokens.astype(f32)
    square = lax.psum(jnp.sum(widened * widened, axis=1), "chan")
    inverse_rms = lax.rsqrt(square / (width_dev * lax.axis_size("chan")) + 1e-05)
    inverse_rms = inverse_rms.reshape(p_block, 1, q_order)

    gain = norm_gain.astype(f32).reshape(1, width_dev)
    factor = first_factor.astype(f32)
    tw_in = twiddle_in.astype(f32)[:, :, None]
    tw_out = twiddle_out.astype(f32).T[:, :, None]
    gate = kernel_gate.transpose(1, 0, 2)
    split = second_factor.reshape(p_order, seq_count, 1, p_block)
    none = jnp.zeros_like(split)
    pair = jnp.stack(
        [jnp.concatenate([split, none], axis=2), jnp.concatenate([none, split], axis=2)]
    ).reshape(2 * p_order, 2 * p_order)

    sent = [
        first_call(tokens, inverse_rms, gain, factor, tw_in, chunk, width)
        for chunk in range(CHUNKS)
    ]
    shape = (seq_count, rows_dev // seq_count, width)
    columns = [
        lax.all_to_all(one.reshape(shape), "seq", split_axis=0, concat_axis=0, tiled=True)
        for one in sent
    ]
    backs = [
        middle_call(one, pair, gate, second_inverse, tw_out, chunk)
        for chunk, one in enumerate(columns)
    ]
    returned = [
        lax.all_to_all(one.reshape(shape), "seq", split_axis=0, concat_axis=0, tiled=True)
        for one in backs
    ]
    out = None
    for chunk, one in enumerate(returned):
        out = last_call(one, first_inverse, out, chunk, width_dev)
    return out


def solution(mesh):
    return jax.shard_map(
        per_device,
        mesh=mesh,
        in_specs=(
            P("seq", "chan"),
            P("chan"),
            P(),
            P("seq", None),
            P(),
            P(None, "seq", "chan"),
            P(),
            P(None, "seq"),
            P(),
        ),
        out_specs=P("seq", "chan"),
        check_vma=False,
    )
```

```python
import jax
import jax.numpy as jnp
from jax import lax
from jax.experimental import pallas as pl
from jax.experimental.pallas import tpu as pltpu
from jax.sharding import PartitionSpec as P

LANES = 128
TILE = 256
VMEM_LIMIT = 48 * 1024 * 1024


def params():
    return pltpu.CompilerParams(
        dimension_semantics=("arbitrary",), vmem_limit_bytes=VMEM_LIMIT
    )


def first_kernel(x_ref, inv_ref, gain_ref, factor_ref, tw_ref, out_ref, tables, held):
    p_block, order, _ = tables.shape
    parts = held.shape[0]

    @pl.when(pl.program_id(0) == 0)
    def _():
        factor = factor_ref[...].astype(jnp.float32)
        for p in range(p_block):
            scaled = factor * inv_ref[p : p + 1, :] * tw_ref[:, p : p + 1]
            tables[p] = scaled.astype(jnp.bfloat16)

    for p in range(p_block):
        result = jnp.dot(
            tables[p], x_ref[p * order : (p + 1) * order, :], preferred_element_type=jnp.float32
        )
        result = result * gain_ref[...].astype(jnp.float32)
        for part in range(parts):
            held[part, pl.ds(p, order, stride=p_block), :] = result[
                :, part * LANES : (part + 1) * LANES
            ]
    for part in range(parts):
        out_ref[:, part * LANES : (part + 1) * LANES] = held[part].astype(jnp.bfloat16)


def first_call(tokens, inv, gain, factor, tw):
    rows, width = tokens.shape
    p_block, order = inv.shape
    return pl.pallas_call(
        first_kernel,
        grid=(width // TILE,),
        in_specs=[
            pl.BlockSpec((rows, TILE), lambda i: (0, i)),
            pl.BlockSpec((p_block, order), lambda i: (0, 0)),
            pl.BlockSpec((1, TILE), lambda i: (0, i)),
            pl.BlockSpec((order, order), lambda i: (0, 0)),
            pl.BlockSpec((order, p_block), lambda i: (0, 0)),
        ],
        out_specs=pl.BlockSpec((rows, TILE), lambda i: (0, i)),
        out_shape=jax.ShapeDtypeStruct((rows, width), jnp.bfloat16),
        scratch_shapes=[
            pltpu.VMEM((p_block, order, order), jnp.bfloat16),
            pltpu.VMEM((TILE // LANES, rows, LANES), jnp.float32),
        ],
        compiler_params=params(),
        cost_estimate=pl.CostEstimate(
            flops=2 * rows * order * width, bytes_accessed=4 * rows * width, transcendentals=0
        ),
        name="first_section",
    )(tokens, inv, gain, factor, tw)


def middle_kernel(v_ref, second_ref, gate_ref, inverse_ref, tw_ref, out_ref, tables, held, gates):
    groups, _, tile = v_ref.shape
    k_block, m_order, _ = tables.shape
    parts = held.shape[0]
    f32 = jnp.float32

    @pl.when(pl.program_id(0) == 0)
    def _():
        inverse = inverse_ref[...].astype(f32)
        for k in range(k_block):
            tables[k] = (inverse * tw_ref[:, k : k + 1]).astype(jnp.bfloat16)

    gate = gate_ref[...].reshape(m_order * k_block, tile)
    for part in range(parts):
        gates[part] = gate[:, part * LANES : (part + 1) * LANES].astype(f32)

    for pair in range(k_block // 2):
        both = v_ref[:, pair * 16 : (pair + 1) * 16, :].astype(f32).reshape(groups, 2, 8, tile)
        for one in range(2):
            k = 2 * pair + one
            values = both[:, one].reshape(groups * 8, tile).astype(jnp.bfloat16)
            gated = jnp.dot(second_ref[...], values, preferred_element_type=f32)
            here = jnp.concatenate(
                [gates[part, pl.ds(k, m_order, stride=k_block), :] for part in range(parts)], axis=1
            )
            gated = (gated * here).astype(jnp.bfloat16)
            back = jnp.dot(tables[k], gated, preferred_element_type=f32)
            for part in range(parts):
                held[part, pl.ds(k, m_order, stride=k_block), :] = back[
                    :, part * LANES : (part + 1) * LANES
                ]
    for part in range(parts):
        out_ref[:, part * LANES : (part + 1) * LANES] = held[part].astype(jnp.bfloat16)


def middle_call(values, second, gate, inverse, tw):
    groups, depth, width = values.shape
    m_order, k_block = tw.shape
    rows = groups * depth
    return pl.pallas_call(
        middle_kernel,
        grid=(width // TILE,),
        in_specs=[
            pl.BlockSpec((groups, depth, TILE), lambda i: (0, 0, i)),
            pl.BlockSpec((m_order, m_order), lambda i: (0, 0)),
            pl.BlockSpec((m_order, k_block, TILE), lambda i: (0, 0, i)),
            pl.BlockSpec((m_order, m_order), lambda i: (0, 0)),
            pl.BlockSpec((m_order, k_block), lambda i: (0, 0)),
        ],
        out_specs=pl.BlockSpec((rows, TILE), lambda i: (0, i)),
        out_shape=jax.ShapeDtypeStruct((rows, width), jnp.bfloat16),
        scratch_shapes=[
            pltpu.VMEM((k_block, m_order, m_order), jnp.bfloat16),
            pltpu.VMEM((TILE // LANES, rows, LANES), jnp.float32),
            pltpu.VMEM((TILE // LANES, rows, LANES), jnp.float32),
        ],
        compiler_params=params(),
        cost_estimate=pl.CostEstimate(
            flops=4 * rows * m_order * width, bytes_accessed=6 * rows * width, transcendentals=0
        ),
        name="middle_section",
    )(values, second, gate, inverse, tw)


def last_kernel(per, v_ref, factor_ref, out_ref):
    groups, depth, width = v_ref.shape
    order = factor_ref.shape[0]
    for part in range(depth // per):
        values = v_ref[:, part * per : (part + 1) * per, :].reshape(order, width)
        out_ref[part * order : (part + 1) * order, :] = jnp.dot(
            factor_ref[...], values, preferred_element_type=jnp.float32
        ).astype(jnp.bfloat16)


def last_call(values, factor):
    groups, depth, width = values.shape
    order = factor.shape[0]
    per = order // groups
    steps = 2
    rows = groups * depth
    return pl.pallas_call(
        lambda *refs: last_kernel(per, *refs),
        grid=(steps,),
        in_specs=[
            pl.BlockSpec((groups, depth // steps, width), lambda i: (0, i, 0)),
            pl.BlockSpec((order, order), lambda i: (0, 0)),
        ],
        out_specs=pl.BlockSpec((rows // steps, width), lambda i: (i, 0)),
        out_shape=jax.ShapeDtypeStruct((rows, width), jnp.bfloat16),
        compiler_params=params(),
        cost_estimate=pl.CostEstimate(
            flops=2 * rows * order * width, bytes_accessed=4 * rows * width, transcendentals=0
        ),
        name="last_section",
    )(values, factor)


def chan_sum(part):
    count = lax.axis_size("chan")
    total = part
    for shift in range(1, count):
        pairs = [(i, (i + shift) % count) for i in range(count)]
        total = total + lax.ppermute(part, "chan", pairs)
    return total


def per_device(
    tokens,
    norm_gain,
    first_factor,
    twiddle_in,
    second_factor,
    kernel_gate,
    second_inverse,
    twiddle_out,
    first_inverse,
):
    f32 = jnp.float32
    seq_count = lax.axis_size("seq")
    rows_dev, width_dev = tokens.shape
    q_order = first_factor.shape[0]
    p_block = rows_dev // q_order

    widened = tokens.reshape(p_block, q_order, width_dev).astype(f32)
    square = chan_sum(jnp.sum(widened * widened, axis=2))
    inverse_rms = lax.rsqrt(square / (width_dev * lax.axis_size("chan")) + 1e-05)

    sent = first_call(
        tokens,
        inverse_rms,
        norm_gain.reshape(1, width_dev),
        first_factor,
        twiddle_in.T.astype(f32),
    )
    shape = (seq_count, rows_dev // seq_count, width_dev)
    sent, tw_out = lax.optimization_barrier((sent.reshape(shape), twiddle_out.astype(f32)))
    columns = lax.all_to_all(sent, "seq", split_axis=0, concat_axis=0, tiled=True)
    back = middle_call(columns, second_factor, kernel_gate, second_inverse, tw_out)
    returned = lax.all_to_all(back.reshape(shape), "seq", split_axis=0, concat_axis=0, tiled=True)
    return last_call(returned, first_inverse)


def solution(mesh):
    return jax.shard_map(
        per_device,
        mesh=mesh,
        in_specs=(
            P("seq", "chan"),
            P("chan"),
            P(),
            P("seq", None),
            P(),
            P(None, "seq", "chan"),
            P(),
            P(None, "seq"),
            P(),
        ),
        out_specs=P("seq", "chan"),
        check_vma=False,
    )
```

```python
import functools

import jax
import jax.numpy as jnp
from jax import lax
from jax.experimental import pallas as pl
from jax.experimental.pallas import tpu as pltpu
from jax.sharding import PartitionSpec as P

LANES = 128
TILE = 256
CUTS = (((4,), (4,), "FR", True), ((1, 3), (1, 3), "FFRR", True))
VMEM_LIMIT = 48 * 1024 * 1024


def params():
    return pltpu.CompilerParams(
        dimension_semantics=("arbitrary",), vmem_limit_bytes=VMEM_LIMIT
    )


def first_kernel(x_ref, inv_ref, gain_ref, factor_ref, tw_ref, out_ref, tables, held):
    p_block, order, _ = tables.shape
    parts = held.shape[0]

    @pl.when(pl.program_id(0) == 0)
    def _():
        factor = factor_ref[...].astype(jnp.float32)
        for p in range(p_block):
            scaled = factor * inv_ref[p : p + 1, :] * tw_ref[:, p : p + 1]
            tables[p] = scaled.astype(jnp.bfloat16)

    for p in range(p_block):
        result = jnp.dot(
            tables[p], x_ref[p * order : (p + 1) * order, :], preferred_element_type=jnp.float32
        )
        result = result * gain_ref[...].astype(jnp.float32)
        for part in range(parts):
            held[part, pl.ds(p, order, stride=p_block), :] = result[
                :, part * LANES : (part + 1) * LANES
            ]
    for part in range(parts):
        out_ref[:, part * LANES : (part + 1) * LANES] = held[part].astype(jnp.bfloat16)


def first_call(tokens, inv, gain, factor, tw, start, tiles):
    rows, _ = tokens.shape
    width = tiles * TILE
    p_block, order = inv.shape
    return pl.pallas_call(
        first_kernel,
        grid=(tiles,),
        in_specs=[
            pl.BlockSpec((rows, TILE), lambda i: (0, start + i)),
            pl.BlockSpec((p_block, order), lambda i: (0, 0)),
            pl.BlockSpec((1, TILE), lambda i: (0, start + i)),
            pl.BlockSpec((order, order), lambda i: (0, 0)),
            pl.BlockSpec((order, p_block), lambda i: (0, 0)),
        ],
        out_specs=pl.BlockSpec((rows, TILE), lambda i: (0, i)),
        out_shape=jax.ShapeDtypeStruct((rows, width), jnp.bfloat16),
        scratch_shapes=[
            pltpu.VMEM((p_block, order, order), jnp.bfloat16),
            pltpu.VMEM((TILE // LANES, rows, LANES), jnp.float32),
        ],
        compiler_params=params(),
        cost_estimate=pl.CostEstimate(
            flops=2 * rows * order * width, bytes_accessed=4 * rows * width, transcendentals=0
        ),
        name="first_section",
    )(tokens, inv, gain, factor, tw)


def middle_kernel(v_ref, second_ref, gate_ref, inverse_ref, tw_ref, *rest):
    out_ref, tables, held, gates = rest[-4:]
    groups, _, tile = v_ref.shape
    k_block, m_order, _ = tables.shape
    parts = held.shape[0]
    f32 = jnp.float32

    @pl.when(pl.program_id(0) == 0)
    def _():
        inverse = inverse_ref[...].astype(f32)
        for k in range(k_block):
            tables[k] = (inverse * tw_ref[:, k : k + 1]).astype(jnp.bfloat16)

    gate = gate_ref[...].reshape(m_order * k_block, tile)
    for part in range(parts):
        gates[part] = gate[:, part * LANES : (part + 1) * LANES].astype(f32)

    for pair in range(k_block // 2):
        both = v_ref[:, pair * 16 : (pair + 1) * 16, :].astype(f32).reshape(groups, 2, 8, tile)
        for one in range(2):
            k = 2 * pair + one
            values = both[:, one].reshape(groups * 8, tile).astype(jnp.bfloat16)
            gated = jnp.dot(second_ref[...], values, preferred_element_type=f32)
            here = jnp.concatenate(
                [gates[part, pl.ds(k, m_order, stride=k_block), :] for part in range(parts)], axis=1
            )
            gated = (gated * here).astype(jnp.bfloat16)
            back = jnp.dot(tables[k], gated, preferred_element_type=f32)
            for part in range(parts):
                held[part, pl.ds(k, m_order, stride=k_block), :] = back[
                    :, part * LANES : (part + 1) * LANES
                ]
    for part in range(parts):
        out_ref[:, part * LANES : (part + 1) * LANES] = held[part].astype(jnp.bfloat16)


def middle_call(values, second, gate, inverse, tw, so_far, at, to, start, tiles, width):
    groups, depth, _ = values.shape
    m_order, k_block = tw.shape
    rows = groups * depth
    in_specs = [
        pl.BlockSpec((groups, depth, TILE), lambda i: (0, 0, at + i)),
        pl.BlockSpec((m_order, m_order), lambda i: (0, 0)),
        pl.BlockSpec((m_order, k_block, TILE), lambda i: (0, 0, start + i)),
        pl.BlockSpec((m_order, m_order), lambda i: (0, 0)),
        pl.BlockSpec((m_order, k_block), lambda i: (0, 0)),
    ]
    operands = [values, second, gate, inverse, tw]
    aliases = {}
    if so_far is not None:
        in_specs.append(pl.BlockSpec(memory_space=pl.ANY))
        aliases = {len(operands): 0}
        operands.append(so_far)
    return pl.pallas_call(
        middle_kernel,
        grid=(tiles,),
        in_specs=in_specs,
        out_specs=pl.BlockSpec((rows, TILE), lambda i: (0, to + i)),
        out_shape=jax.ShapeDtypeStruct((rows, width), jnp.bfloat16),
        input_output_aliases=aliases,
        scratch_shapes=[
            pltpu.VMEM((k_block, m_order, m_order), jnp.bfloat16),
            pltpu.VMEM((TILE // LANES, rows, LANES), jnp.float32),
            pltpu.VMEM((TILE // LANES, rows, LANES), jnp.float32),
        ],
        compiler_params=params(),
        cost_estimate=pl.CostEstimate(
            flops=4 * rows * m_order * tiles * TILE,
            bytes_accessed=6 * rows * tiles * TILE,
            transcendentals=0,
        ),
        name="middle_section",
    )(*operands)


def last_kernel(per, v_ref, factor_ref, *rest):
    out_ref = rest[-1]
    groups, depth, width = v_ref.shape
    order = factor_ref.shape[0]
    for part in range(depth // per):
        values = v_ref[:, part * per : (part + 1) * per, :].reshape(order, width)
        out_ref[part * order : (part + 1) * order, :] = jnp.dot(
            factor_ref[...], values, preferred_element_type=jnp.float32
        ).astype(jnp.bfloat16)


def last_call(values, factor, so_far, start, full_width):
    groups, depth, width = values.shape
    order = factor.shape[0]
    per = order // groups
    rows = groups * depth
    whole = width == full_width
    steps = 2 if whole else width // TILE
    if whole:
        in_block = pl.BlockSpec((groups, depth // steps, width), lambda i: (0, i, 0))
        out_block = pl.BlockSpec((rows // steps, width), lambda i: (i, 0))
    else:
        in_block = pl.BlockSpec((groups, depth, TILE), lambda i: (0, 0, i))
        out_block = pl.BlockSpec((rows, TILE), lambda i: (0, start + i))
    in_specs = [in_block, pl.BlockSpec((order, order), lambda i: (0, 0))]
    operands = [values, factor]
    aliases = {}
    if so_far is not None:
        in_specs.append(pl.BlockSpec(memory_space=pl.ANY))
        aliases = {len(operands): 0}
        operands.append(so_far)
    return pl.pallas_call(
        functools.partial(last_kernel, per),
        grid=(steps,),
        in_specs=in_specs,
        out_specs=out_block,
        out_shape=pltpu.HBM((rows, full_width), jnp.bfloat16),
        input_output_aliases=aliases,
        compiler_params=params(),
        cost_estimate=pl.CostEstimate(
            flops=2 * rows * order * width, bytes_accessed=4 * rows * width, transcendentals=0
        ),
        name="last_section",
    )(*operands)


def chan_sum(part):
    count = lax.axis_size("chan")
    total = part
    for shift in range(1, count):
        pairs = [(i, (i + shift) % count) for i in range(count)]
        total = total + lax.ppermute(part, "chan", pairs)
    return total


def per_device(
    tokens,
    norm_gain,
    first_factor,
    twiddle_in,
    second_factor,
    kernel_gate,
    second_inverse,
    twiddle_out,
    first_inverse,
):
    f32 = jnp.float32
    seq_count = lax.axis_size("seq")
    rows_dev, width_dev = tokens.shape
    q_order = first_factor.shape[0]
    p_block = rows_dev // q_order

    widened = tokens.reshape(p_block, q_order, width_dev).astype(f32)
    square = chan_sum(jnp.sum(widened * widened, axis=2))
    inverse_rms = lax.rsqrt(square / (width_dev * lax.axis_size("chan")) + 1e-05)

    gain = norm_gain.reshape(1, width_dev)
    tw_in = twiddle_in.T.astype(f32)
    inverse_rms, tw_out = lax.optimization_barrier((inverse_rms, twiddle_out.astype(f32)))

    def exchange(values):
        values = values.reshape(seq_count, rows_dev // seq_count, -1)
        return lax.all_to_all(values, "seq", split_axis=0, concat_axis=0, tiled=True)

    def cut(forward, backward, order, one_by_one, operands):
        tokens, inv, gain, first_factor, tw_in, second, gate, inverse, tw_out, last = operands
        arrived = []
        returned = []
        forward = list(forward)
        backward = list(backward)
        for step in order:
            if step == "F":
                tiles = forward.pop(0)
                start = arrived[-1][1] if arrived else 0
                values = exchange(first_call(tokens, inv, gain, first_factor, tw_in, start, tiles))
            else:
                tiles = backward.pop(0)
                start = returned[-1][1] if returned else 0
                values = None
                for low, high, columns in arrived:
                    first, end = max(low, start), min(high, start + tiles)
                    if first < end:
                        values = middle_call(
                            columns, second, gate, inverse, tw_out, values,
                            first - low, first - start, first, end - first, tiles * TILE,
                        )
                values = exchange(values)
            if one_by_one:
                values, inv, tw_out = lax.optimization_barrier((values, inv, tw_out))
            (arrived if step == "F" else returned).append((start, start + tiles, values))
        starts, _, values = zip(*returned)
        if one_by_one:
            values = lax.optimization_barrier(values)
        out = None
        for start, one in zip(starts, values):
            out = last_call(one, last, out, start, width_dev)
        return out

    operands = (
        tokens, inverse_rms, gain, first_factor, tw_in,
        second_factor, kernel_gate, second_inverse, tw_out, first_inverse,
    )
    return lax.cond(
        lax.axis_index("chan") % 2 == 0,
        functools.partial(cut, *CUTS[0]),
        functools.partial(cut, *CUTS[1]),
        operands,
    )


def solution(mesh):
    return jax.shard_map(
        per_device,
        mesh=mesh,
        in_specs=(
            P("seq", "chan"),
            P("chan"),
            P(),
            P("seq", None),
            P(),
            P(None, "seq", "chan"),
            P(),
            P(None, "seq"),
            P(),
        ),
        out_specs=P("seq", "chan"),
        check_vma=False,
    )
```

```python
import functools

import jax
import jax.numpy as jnp
from jax import lax
from jax.experimental import pallas as pl
from jax.experimental.pallas import tpu as pltpu
from jax.sharding import PartitionSpec as P

LANES = 128
TILE = 256
CUTS = (((4,), (4,), "FR", True), ((1, 1, 2), (4,), "FFFR", True))
VMEM_LIMIT = 48 * 1024 * 1024


def params(axes=1):
    return pltpu.CompilerParams(
        dimension_semantics=("arbitrary",) * axes, vmem_limit_bytes=VMEM_LIMIT
    )


def first_kernel(x_ref, inv_ref, gain_ref, factor_ref, tw_ref, out_ref, tables, held):
    p_block, order, _ = tables.shape
    parts = held.shape[0]

    @pl.when(pl.program_id(0) == 0)
    def _():
        factor = factor_ref[...].astype(jnp.float32)
        for p in range(p_block):
            scaled = factor * inv_ref[p : p + 1, :] * tw_ref[:, p : p + 1]
            tables[p] = scaled.astype(jnp.bfloat16)

    for p in range(p_block):
        result = jnp.dot(
            tables[p], x_ref[p * order : (p + 1) * order, :], preferred_element_type=jnp.float32
        )
        result = result * gain_ref[...].astype(jnp.float32)
        for part in range(parts):
            held[part, pl.ds(p, order, stride=p_block), :] = result[
                :, part * LANES : (part + 1) * LANES
            ]
    for part in range(parts):
        out_ref[:, part * LANES : (part + 1) * LANES] = held[part].astype(jnp.bfloat16)


def first_call(tokens, inv, gain, factor, tw, start, tiles):
    rows, _ = tokens.shape
    width = tiles * TILE
    p_block, order = inv.shape
    return pl.pallas_call(
        first_kernel,
        grid=(tiles,),
        in_specs=[
            pl.BlockSpec((rows, TILE), lambda i: (0, start + i)),
            pl.BlockSpec((p_block, order), lambda i: (0, 0)),
            pl.BlockSpec((1, TILE), lambda i: (0, start + i)),
            pl.BlockSpec((order, order), lambda i: (0, 0)),
            pl.BlockSpec((order, p_block), lambda i: (0, 0)),
        ],
        out_specs=pl.BlockSpec((rows, TILE), lambda i: (0, i)),
        out_shape=jax.ShapeDtypeStruct((rows, width), jnp.bfloat16),
        scratch_shapes=[
            pltpu.VMEM((p_block, order, order), jnp.bfloat16),
            pltpu.VMEM((TILE // LANES, rows, LANES), jnp.float32),
        ],
        compiler_params=params(),
        cost_estimate=pl.CostEstimate(
            flops=2 * rows * order * width, bytes_accessed=4 * rows * width, transcendentals=0
        ),
        name="first_section",
    )(tokens, inv, gain, factor, tw)


def middle_kernel(v_ref, second_ref, gate_ref, inverse_ref, tw_ref, *rest):
    out_ref, tables, held, gates = rest[-4:]
    groups, _, tile = v_ref.shape
    k_block, m_order, _ = tables.shape
    parts = held.shape[0]
    f32 = jnp.float32

    @pl.when(pl.program_id(0) == 0)
    def _():
        inverse = inverse_ref[...].astype(f32)
        for k in range(k_block):
            tables[k] = (inverse * tw_ref[:, k : k + 1]).astype(jnp.bfloat16)

    gate = gate_ref[...].reshape(m_order * k_block, tile)
    for part in range(parts):
        gates[part] = gate[:, part * LANES : (part + 1) * LANES].astype(f32)

    for pair in range(k_block // 2):
        both = v_ref[:, pair * 16 : (pair + 1) * 16, :].astype(f32).reshape(groups, 2, 8, tile)
        for one in range(2):
            k = 2 * pair + one
            values = both[:, one].reshape(groups * 8, tile).astype(jnp.bfloat16)
            gated = jnp.dot(second_ref[...], values, preferred_element_type=f32)
            here = jnp.concatenate(
                [gates[part, pl.ds(k, m_order, stride=k_block), :] for part in range(parts)], axis=1
            )
            gated = (gated * here).astype(jnp.bfloat16)
            back = jnp.dot(tables[k], gated, preferred_element_type=f32)
            for part in range(parts):
                held[part, pl.ds(k, m_order, stride=k_block), :] = back[
                    :, part * LANES : (part + 1) * LANES
                ]
    for part in range(parts):
        out_ref[:, part * LANES : (part + 1) * LANES] = held[part].astype(jnp.bfloat16)


def middle_call(values, second, gate, inverse, tw, so_far, at, to, start, tiles, width):
    groups, depth, _ = values.shape
    m_order, k_block = tw.shape
    rows = groups * depth
    in_specs = [
        pl.BlockSpec((groups, depth, TILE), lambda i: (0, 0, at + i)),
        pl.BlockSpec((m_order, m_order), lambda i: (0, 0)),
        pl.BlockSpec((m_order, k_block, TILE), lambda i: (0, 0, start + i)),
        pl.BlockSpec((m_order, m_order), lambda i: (0, 0)),
        pl.BlockSpec((m_order, k_block), lambda i: (0, 0)),
    ]
    operands = [values, second, gate, inverse, tw]
    aliases = {}
    if so_far is not None:
        in_specs.append(pl.BlockSpec(memory_space=pl.ANY))
        aliases = {len(operands): 0}
        operands.append(so_far)
    return pl.pallas_call(
        middle_kernel,
        grid=(tiles,),
        in_specs=in_specs,
        out_specs=pl.BlockSpec((rows, TILE), lambda i: (0, to + i)),
        out_shape=jax.ShapeDtypeStruct((rows, width), jnp.bfloat16),
        input_output_aliases=aliases,
        scratch_shapes=[
            pltpu.VMEM((k_block, m_order, m_order), jnp.bfloat16),
            pltpu.VMEM((TILE // LANES, rows, LANES), jnp.float32),
            pltpu.VMEM((TILE // LANES, rows, LANES), jnp.float32),
        ],
        compiler_params=params(),
        cost_estimate=pl.CostEstimate(
            flops=4 * rows * m_order * tiles * TILE,
            bytes_accessed=6 * rows * tiles * TILE,
            transcendentals=0,
        ),
        name="middle_section",
    )(*operands)


def last_kernel(per, v_ref, factor_ref, *rest):
    out_ref = rest[-1]
    groups, depth, width = v_ref.shape
    order = factor_ref.shape[0]
    for part in range(depth // per):
        values = v_ref[:, part * per : (part + 1) * per, :].reshape(order, width)
        out_ref[part * order : (part + 1) * order, :] = jnp.dot(
            factor_ref[...], values, preferred_element_type=jnp.float32
        ).astype(jnp.bfloat16)


def last_call(values, factor, so_far, start, full_width):
    groups, depth, width = values.shape
    order = factor.shape[0]
    per = order // groups
    rows = groups * depth
    whole = width == full_width
    tile = width if whole else TILE
    in_block = pl.BlockSpec((groups, depth // 2, tile), lambda i, j: (0, j, i))
    out_block = pl.BlockSpec((rows // 2, tile), lambda i, j: (j, start + i))
    in_specs = [in_block, pl.BlockSpec((order, order), lambda i, j: (0, 0))]
    operands = [values, factor]
    aliases = {}
    if so_far is not None:
        in_specs.append(pl.BlockSpec(memory_space=pl.ANY))
        aliases = {len(operands): 0}
        operands.append(so_far)
    return pl.pallas_call(
        functools.partial(last_kernel, per),
        grid=(width // tile, 2),
        in_specs=in_specs,
        out_specs=out_block,
        out_shape=pltpu.HBM((rows, full_width), jnp.bfloat16),
        input_output_aliases=aliases,
        compiler_params=params(2),
        cost_estimate=pl.CostEstimate(
            flops=2 * rows * order * width, bytes_accessed=4 * rows * width, transcendentals=0
        ),
        name="last_section",
    )(*operands)


def chan_sum(part):
    count = lax.axis_size("chan")
    total = part
    for shift in range(1, count):
        pairs = [(i, (i + shift) % count) for i in range(count)]
        total = total + lax.ppermute(part, "chan", pairs)
    return total


def per_device(
    tokens,
    norm_gain,
    first_factor,
    twiddle_in,
    second_factor,
    kernel_gate,
    second_inverse,
    twiddle_out,
    first_inverse,
):
    f32 = jnp.float32
    seq_count = lax.axis_size("seq")
    rows_dev, width_dev = tokens.shape
    q_order = first_factor.shape[0]
    p_block = rows_dev // q_order

    widened = tokens.reshape(p_block, q_order, width_dev).astype(f32)
    square = chan_sum(jnp.sum(widened * widened, axis=2))
    inverse_rms = lax.rsqrt(square / (width_dev * lax.axis_size("chan")) + 1e-05)

    gain = norm_gain.reshape(1, width_dev)
    tw_in = twiddle_in.T.astype(f32)
    inverse_rms, tw_out = lax.optimization_barrier((inverse_rms, twiddle_out.astype(f32)))

    def exchange(values):
        values = values.reshape(seq_count, rows_dev // seq_count, -1)
        return lax.all_to_all(values, "seq", split_axis=0, concat_axis=0, tiled=True)

    def cut(forward, backward, order, one_by_one, operands):
        tokens, inv, gain, first_factor, tw_in, second, gate, inverse, tw_out, last = operands
        arrived = []
        returned = []
        forward = list(forward)
        backward = list(backward)
        for step in order:
            if step == "F":
                tiles = forward.pop(0)
                start = arrived[-1][1] if arrived else 0
                values = exchange(first_call(tokens, inv, gain, first_factor, tw_in, start, tiles))
            else:
                tiles = backward.pop(0)
                start = returned[-1][1] if returned else 0
                values = None
                for low, high, columns in arrived:
                    first, end = max(low, start), min(high, start + tiles)
                    if first < end:
                        values = middle_call(
                            columns, second, gate, inverse, tw_out, values,
                            first - low, first - start, first, end - first, tiles * TILE,
                        )
                values = exchange(values)
            if one_by_one:
                values, inv, tw_out = lax.optimization_barrier((values, inv, tw_out))
            (arrived if step == "F" else returned).append((start, start + tiles, values))
        starts, _, values = zip(*returned)
        if one_by_one:
            values = lax.optimization_barrier(values)
        out = None
        for start, one in zip(starts, values):
            out = last_call(one, last, out, start, width_dev)
        return out

    operands = (
        tokens, inverse_rms, gain, first_factor, tw_in,
        second_factor, kernel_gate, second_inverse, tw_out, first_inverse,
    )
    return lax.cond(
        lax.axis_index("chan") % 2 == 0,
        functools.partial(cut, *CUTS[0]),
        functools.partial(cut, *CUTS[1]),
        operands,
    )


def solution(mesh):
    return jax.shard_map(
        per_device,
        mesh=mesh,
        in_specs=(
            P("seq", "chan"),
            P("chan"),
            P(),
            P("seq", None),
            P(),
            P(None, "seq", "chan"),
            P(),
            P(None, "seq"),
            P(),
        ),
        out_specs=P("seq", "chan"),
        check_vma=False,
    )
```

```python
import functools

import jax
import jax.numpy as jnp
from jax import lax
from jax.experimental import pallas as pl
from jax.experimental.pallas import tpu as pltpu
from jax.sharding import PartitionSpec as P

LANES = 128
TILE = 256
CUTS = (((4,), (4,), "FR", True), ((1, 1, 2), (4,), "FFFR", True))
VMEM_LIMIT = 48 * 1024 * 1024


def params(axes=1):
    return pltpu.CompilerParams(
        dimension_semantics=("arbitrary",) * axes, vmem_limit_bytes=VMEM_LIMIT
    )


def first_kernel(x_ref, inv_ref, gain_ref, factor_ref, tw_ref, out_ref, tables, held):
    p_block, order, _ = tables.shape
    parts = held.shape[0]

    @pl.when(pl.program_id(0) == 0)
    def _():
        factor = factor_ref[...].astype(jnp.float32)
        for p in range(p_block):
            scaled = factor * inv_ref[p : p + 1, :] * tw_ref[:, p : p + 1]
            tables[p] = scaled.astype(jnp.bfloat16)

    for p in range(p_block):
        result = jnp.dot(
            tables[p], x_ref[p * order : (p + 1) * order, :], preferred_element_type=jnp.float32
        )
        result = result * gain_ref[...].astype(jnp.float32)
        for part in range(parts):
            held[part, pl.ds(p, order, stride=p_block), :] = result[
                :, part * LANES : (part + 1) * LANES
            ]
    for part in range(parts):
        out_ref[:, part * LANES : (part + 1) * LANES] = held[part].astype(jnp.bfloat16)


def first_call(tokens, inv, gain, factor, tw, start, tiles):
    rows, _ = tokens.shape
    width = tiles * TILE
    p_block, order = inv.shape
    return pl.pallas_call(
        first_kernel,
        grid=(tiles,),
        in_specs=[
            pl.BlockSpec((rows, TILE), lambda i: (0, start + i)),
            pl.BlockSpec((p_block, order), lambda i: (0, 0)),
            pl.BlockSpec((1, TILE), lambda i: (0, start + i)),
            pl.BlockSpec((order, order), lambda i: (0, 0)),
            pl.BlockSpec((order, p_block), lambda i: (0, 0)),
        ],
        out_specs=pl.BlockSpec((rows, TILE), lambda i: (0, i)),
        out_shape=jax.ShapeDtypeStruct((rows, width), jnp.bfloat16),
        scratch_shapes=[
            pltpu.VMEM((p_block, order, order), jnp.bfloat16),
            pltpu.VMEM((TILE // LANES, rows, LANES), jnp.float32),
        ],
        compiler_params=params(),
        cost_estimate=pl.CostEstimate(
            flops=2 * rows * order * width, bytes_accessed=4 * rows * width, transcendentals=0
        ),
        name="first_section",
    )(tokens, inv, gain, factor, tw)


def middle_kernel(spans, *refs):
    sources = refs[: len(spans)]
    others = refs[len(spans) :]
    if len(spans) == 1:
        middle_tile(sources[0], *others)
        return
    step = pl.program_id(0)
    for (low, high), source in zip(spans, sources):
        pl.when(jnp.logical_and(step >= low, step < high))(
            functools.partial(middle_tile, source, *others)
        )


def middle_tile(v_ref, second_ref, gate_ref, inverse_ref, tw_ref, out_ref, tables, held, gates):
    groups, _, tile = v_ref.shape
    k_block, m_order, _ = tables.shape
    parts = held.shape[0]
    f32 = jnp.float32

    @pl.when(pl.program_id(0) == 0)
    def _():
        inverse = inverse_ref[...].astype(f32)
        for k in range(k_block):
            tables[k] = (inverse * tw_ref[:, k : k + 1]).astype(jnp.bfloat16)

    gate = gate_ref[...].reshape(m_order * k_block, tile)
    for part in range(parts):
        gates[part] = gate[:, part * LANES : (part + 1) * LANES].astype(f32)

    for pair in range(k_block // 2):
        both = v_ref[:, pair * 16 : (pair + 1) * 16, :].astype(f32).reshape(groups, 2, 8, tile)
        for one in range(2):
            k = 2 * pair + one
            values = both[:, one].reshape(groups * 8, tile).astype(jnp.bfloat16)
            gated = jnp.dot(second_ref[...], values, preferred_element_type=f32)
            here = jnp.concatenate(
                [gates[part, pl.ds(k, m_order, stride=k_block), :] for part in range(parts)], axis=1
            )
            gated = (gated * here).astype(jnp.bfloat16)
            back = jnp.dot(tables[k], gated, preferred_element_type=f32)
            for part in range(parts):
                held[part, pl.ds(k, m_order, stride=k_block), :] = back[
                    :, part * LANES : (part + 1) * LANES
                ]
    for part in range(parts):
        out_ref[:, part * LANES : (part + 1) * LANES] = held[part].astype(jnp.bfloat16)


def middle_call(parts, second, gate, inverse, tw, start, tiles):
    groups, depth, _ = parts[0][3].shape
    m_order, k_block = tw.shape
    rows = groups * depth
    in_specs = []
    for low, count, at, _ in parts:
        in_specs.append(
            pl.BlockSpec(
                (groups, depth, TILE),
                lambda i, low=low, count=count, at=at: (0, 0, at + jnp.clip(i - low, 0, count - 1)),
            )
        )
    in_specs += [
        pl.BlockSpec((m_order, m_order), lambda i: (0, 0)),
        pl.BlockSpec((m_order, k_block, TILE), lambda i: (0, 0, start + i)),
        pl.BlockSpec((m_order, m_order), lambda i: (0, 0)),
        pl.BlockSpec((m_order, k_block), lambda i: (0, 0)),
    ]
    operands = [part[3] for part in parts] + [second, gate, inverse, tw]
    spans = tuple((low, low + count) for low, count, _, _ in parts)
    return pl.pallas_call(
        functools.partial(middle_kernel, spans),
        grid=(tiles,),
        in_specs=in_specs,
        out_specs=pl.BlockSpec((rows, TILE), lambda i: (0, i)),
        out_shape=jax.ShapeDtypeStruct((rows, tiles * TILE), jnp.bfloat16),
        scratch_shapes=[
            pltpu.VMEM((k_block, m_order, m_order), jnp.bfloat16),
            pltpu.VMEM((TILE // LANES, rows, LANES), jnp.float32),
            pltpu.VMEM((TILE // LANES, rows, LANES), jnp.float32),
        ],
        compiler_params=params(),
        cost_estimate=pl.CostEstimate(
            flops=4 * rows * m_order * tiles * TILE,
            bytes_accessed=6 * rows * tiles * TILE,
            transcendentals=0,
        ),
        name="middle_section",
    )(*operands)


def last_kernel(per, v_ref, factor_ref, *rest):
    out_ref = rest[-1]
    groups, depth, width = v_ref.shape
    order = factor_ref.shape[0]
    for part in range(depth // per):
        values = v_ref[:, part * per : (part + 1) * per, :].reshape(order, width)
        out_ref[part * order : (part + 1) * order, :] = jnp.dot(
            factor_ref[...], values, preferred_element_type=jnp.float32
        ).astype(jnp.bfloat16)


def last_call(values, factor, so_far, start, full_width):
    groups, depth, width = values.shape
    order = factor.shape[0]
    per = order // groups
    rows = groups * depth
    whole = width == full_width
    tile = width if whole else TILE
    in_block = pl.BlockSpec((groups, depth // 2, tile), lambda i, j: (0, j, i))
    out_block = pl.BlockSpec((rows // 2, tile), lambda i, j: (j, start + i))
    in_specs = [in_block, pl.BlockSpec((order, order), lambda i, j: (0, 0))]
    operands = [values, factor]
    aliases = {}
    if so_far is not None:
        in_specs.append(pl.BlockSpec(memory_space=pl.ANY))
        aliases = {len(operands): 0}
        operands.append(so_far)
    return pl.pallas_call(
        functools.partial(last_kernel, per),
        grid=(width // tile, 2),
        in_specs=in_specs,
        out_specs=out_block,
        out_shape=pltpu.HBM((rows, full_width), jnp.bfloat16),
        input_output_aliases=aliases,
        compiler_params=params(2),
        cost_estimate=pl.CostEstimate(
            flops=2 * rows * order * width, bytes_accessed=4 * rows * width, transcendentals=0
        ),
        name="last_section",
    )(*operands)


def chan_sum(part):
    count = lax.axis_size("chan")
    total = part
    for shift in range(1, count):
        pairs = [(i, (i + shift) % count) for i in range(count)]
        total = total + lax.ppermute(part, "chan", pairs)
    return total


def per_device(
    tokens,
    norm_gain,
    first_factor,
    twiddle_in,
    second_factor,
    kernel_gate,
    second_inverse,
    twiddle_out,
    first_inverse,
):
    f32 = jnp.float32
    seq_count = lax.axis_size("seq")
    rows_dev, width_dev = tokens.shape
    q_order = first_factor.shape[0]
    p_block = rows_dev // q_order

    widened = tokens.reshape(p_block, q_order, width_dev).astype(f32)
    square = chan_sum(jnp.sum(widened * widened, axis=2))
    inverse_rms = lax.rsqrt(square / (width_dev * lax.axis_size("chan")) + 1e-05)

    gain = norm_gain.reshape(1, width_dev)
    tw_in = twiddle_in.T.astype(f32)
    inverse_rms, tw_out = lax.optimization_barrier((inverse_rms, twiddle_out.astype(f32)))

    def exchange(values):
        values = values.reshape(seq_count, rows_dev // seq_count, -1)
        return lax.all_to_all(values, "seq", split_axis=0, concat_axis=0, tiled=True)

    def cut(forward, backward, order, one_by_one, operands):
        tokens, inv, gain, first_factor, tw_in, second, gate, inverse, tw_out, last = operands
        arrived = []
        returned = []
        forward = list(forward)
        backward = list(backward)
        for step in order:
            if step == "F":
                tiles = forward.pop(0)
                start = arrived[-1][1] if arrived else 0
                values = exchange(first_call(tokens, inv, gain, first_factor, tw_in, start, tiles))
            else:
                tiles = backward.pop(0)
                start = returned[-1][1] if returned else 0
                parts = []
                for low, high, columns in arrived:
                    first, end = max(low, start), min(high, start + tiles)
                    if first < end:
                        parts.append((first - start, end - first, first - low, columns))
                values = middle_call(parts, second, gate, inverse, tw_out, start, tiles)
                values = exchange(values)
            if one_by_one:
                values, inv, tw_out = lax.optimization_barrier((values, inv, tw_out))
            (arrived if step == "F" else returned).append((start, start + tiles, values))
        starts, _, values = zip(*returned)
        if one_by_one:
            values = lax.optimization_barrier(values)
        out = None
        for start, one in zip(starts, values):
            out = last_call(one, last, out, start, width_dev)
        return out

    operands = (
        tokens, inverse_rms, gain, first_factor, tw_in,
        second_factor, kernel_gate, second_inverse, tw_out, first_inverse,
    )
    return lax.cond(
        lax.axis_index("chan") % 2 == 0,
        functools.partial(cut, *CUTS[0]),
        functools.partial(cut, *CUTS[1]),
        operands,
    )


def solution(mesh):
    return jax.shard_map(
        per_device,
        mesh=mesh,
        in_specs=(
            P("seq", "chan"),
            P("chan"),
            P(),
            P("seq", None),
            P(),
            P(None, "seq", "chan"),
            P(),
            P(None, "seq"),
            P(),
        ),
        out_specs=P("seq", "chan"),
        check_vma=False,
    )
```
